256 devices in a mesh: shot: 32 (over y, z_hi, x), rcv: 8 (over z_lo, core).
Axes of the slice: x: 4, y: 4, z: 8 (z_hi: 2, z_lo: 4; z = z_hi * 4 + z_lo), core: 2. Of those that a mesh axis runs over, the one named last changes fastest.
Arguments:
- data: bfloat16 [2, 8, 4096, 4096], P(None, None, 'shot', 'rcv'), may hold values from -3 to 3
- inverse_wavelet: float32 [2, 8], replicated, may hold values from -1.5 to 1.5
- panel_blocks: int32 [2], replicated, may hold values from 0 to 31, as said below
Outputs:
- multiples: bfloat16 [16, 4096, 4096], P(None, 'shot', 'rcv')
The draws below stay inside these ranges and needn't reach their ends.
Inputs may be any that keep to these rules, and one draw needn't show every extreme that they name: `panel_blocks`: the panels' blocks are distinct, and one of them is always the last block, 31.
All inputs are finite; a program needn't handle non-finite values.
Results may differ from the reference program's by a relative error of at most 0.001.
Values may be sent and summed in bfloat16 or wider, within the bound.
A program may use at most 64 MiB of HBM per device.

```python
import math
import jax
import jax.numpy as jnp
from jax import lax

NF = 8
SHOT_DEV = 128
NPANEL = 2
SHOTS = 4096
BLOCKS = 32


def draw_panel_blocks(key, part):
    key = jax.random.fold_in(key, 7)
    first_key, second_key = jax.random.split(key)
    order = jax.random.permutation(first_key, BLOCKS - 1)[:NPANEL].astype(jnp.int32)
    place = jax.random.randint(second_key, (), 0, NPANEL)
    return jnp.where(jnp.arange(NPANEL) == place, BLOCKS - 1, order).astype(jnp.int32)


def level_of(key, dims, cuts, low, top_value):
    loudness = 1.0
    for dim, blocks in cuts:
        heights = jax.random.uniform(jax.random.fold_in(jax.random.fold_in(key, 6), dim), (blocks,), jnp.float32, low / len(cuts), top_value / len(cuts))
        loudness = loudness * jnp.repeat(jnp.exp(heights), dims[dim] // blocks).reshape((-1,) + (1,) * (len(dims) - 1 - dim))
    return loudness


def gaussian(own_key, dims, spread, reach, cuts=(), held_as=jnp.bfloat16):
    array = spread * jax.random.normal(own_key, dims, jnp.float32)
    if cuts:
        array = array * level_of(own_key, dims, cuts, -0.22, 0.18)
    return jnp.clip(array, -reach, reach).astype(held_as)


def setup_inputs(seed: int = 0) -> dict:
    seeds = jax.random.split(jax.random.key(seed), 4)
    data = gaussian(seeds[0], (2, NF, SHOTS, SHOTS), ((2 * NPANEL * SHOT_DEV) ** -0.25), 3.0, ((2, 32), (3, 8)))
    inverse_wavelet = jnp.clip(jax.random.uniform(seeds[1], (2, NF), jnp.float32, -1.5, 1.5), -1.5, 1.5)
    panel_blocks = draw_panel_blocks(jax.random.fold_in(seeds[3], 71), 0)
    return {"data": data, "inverse_wavelet": inverse_wavelet, "panel_blocks": panel_blocks}


def finish(product, inverse_wavelet):
    nf = product.shape[1]
    nt = 2 * nf
    wavefield_real = inverse_wavelet[0][:, None, None]
    wave_im = inverse_wavelet[1][:, None, None]
    scaled_real = wavefield_real * product[0] - wave_im * product[1]
    scaled_imaginary = wavefield_real * product[1] + wave_im * product[0]
    times = jnp.arange(nt, dtype=jnp.float32)
    freqs = jnp.arange(nf, dtype=jnp.float32) + 1.0
    phase = 2.0 * math.pi * times[:, None] * freqs[None, :] / nt
    cosine_factor = jnp.cos(phase)
    sine_factor = jnp.sin(phase)
    first_panel = jnp.einsum("vj,jbw->vbw", cosine_factor, scaled_real, precision=lax.Precision.HIGHEST)
    second_panel = jnp.einsum("vj,jbw->vbw", sine_factor, scaled_imaginary, precision=lax.Precision.HIGHEST)
    return (first_panel - second_panel) * (nf ** -0.5)


def reference(data, inverse_wavelet, panel_blocks):
    shots = data.shape[2]
    nblock = shots // SHOT_DEV
    rights = []
    columns = []
    for panel in range(NPANEL):
        start = (panel_blocks[panel] * SHOT_DEV).astype(jnp.int32)
        rows = lax.dynamic_slice_in_dim(data, start, SHOT_DEV, 2)
        rights.append(jnp.concatenate([rows[0], rows[1]], axis=1).astype(jnp.float32))
        columns.append(lax.dynamic_slice_in_dim(data, start, SHOT_DEV, 3))

    def one_block(index):
        begin = (index * SHOT_DEV).astype(jnp.int32)
        total = jnp.zeros((2, data.shape[1], SHOT_DEV, shots), jnp.float32)
        for panel in range(NPANEL):
            piece = lax.dynamic_slice_in_dim(columns[panel], begin, SHOT_DEV, 2)
            left = jnp.stack([jnp.concatenate([piece[0], -piece[1]], axis=-1),
                              jnp.concatenate([piece[1], piece[0]], axis=-1)]).astype(jnp.float32)
            total = total + jnp.einsum("cfsk,fkr->cfsr", left, rights[panel])
        return finish(total, inverse_wavelet).astype(jnp.bfloat16)

    block_list = lax.map(one_block, jnp.arange(nblock, dtype=jnp.int32))
    return jnp.transpose(block_list, (1, 0, 2, 3)).reshape(block_list.shape[1], shots, shots)
```

```python
import functools
import math

import jax
import jax.numpy as jnp
from jax import lax
from jax.experimental import pallas as pl
from jax.experimental.pallas import tpu as pltpu
from jax.sharding import PartitionSpec as P

MESH = pl.DeviceIdType.MESH
LAST = 31
NF, SIDE, LANES = 8, 128, 128
PIECES = 4
COLS = 4
STEPS = ((1, 0), (0, 1), (-1, 0), (0, -1))

TREE = (
    (0, 0, 0), (1, 0, 1), (1, 0, 3), (1, 0, 0), (2, 0, 0), (1, 1, 2), (1, 1, 0), (1, 3, 2),
    (1, 1, 1), (2, 0, 3), (2, 3, 0), (1, 2, 2), (1, 2, 0), (2, 1, 0), (2, 2, 0),
)
OTHER = (
    ((1, 3), 2, (
        (1, 3, 0), (1, 3, 1), (1, 3, 3), (1, 3, 2), (0, 3, 1), (0, 3, 2), (1, 2, 0), (1, 2, 2),
        (1, 2, 3), (2, 3, 1), (0, 2, 2), (0, 0, 2), (2, 2, 3), (0, 2, 3), (3, 2, 3),
    )),
    ((1, 0), 1, (
        (1, 0, 0), (1, 0, 3), (1, 0, 1), (1, 0, 2), (1, 3, 2), (1, 1, 2), (1, 3, 0), (1, 3, 3),
        (2, 0, 1), (0, 0, 2), (0, 1, 2), (0, 3, 3), (2, 3, 3), (2, 3, 0), (2, 2, 0),
    )),
)
CROSS = 2


def tables(root, edges, base):
    depth = {root: base}
    while len(depth) < 16:
        for x, y, d in edges:
            if (x, y) in depth:
                there = ((x + STEPS[d][0]) % 4, (y + STEPS[d][1]) % 4)
                depth.setdefault(there, depth[(x, y)] + 1)
    masks = [sum(1 << (x * 4 + y) for x, y, d in edges if d == way) for way in range(4)]
    bits = [
        sum(1 << (x * 4 + y) for (x, y), v in depth.items() if (v >> i) & 1) for i in range(4)
    ]
    return masks, bits


HOME = tables((0, 0), TREE, 0)
AWAY = [tables(root, edges, base + CROSS) for root, base, edges in OTHER]


def turned(x, y, times):
    for _ in range(times % 4):
        x, y = -y, x
    return (x + 4) % 4, (y + 4) % 4


def bit(mask, place):
    return (mask >> place) & 1


def place_of(block):
    return block % 4, block // 8, (block // 4) % 2


def gather_kernel(block, data, rows, cols, row_recv, row_send, col_recv, col_send, own_sem):
    shot, rcv = lax.axis_index("shot"), lax.axis_index("rcv")
    x, half, y = shot % 4, (shot // 4) % 2, shot // 8
    run, core = rcv // 2, rcv % 2

    def at(px, py, ph):
        return (py * 2 + ph) * 4 + px

    beside = [(at((x + a + 4) % 4, (y + b + 4) % 4, half), rcv) for a, b in STEPS]
    across = (at(x, y, 1 - half), rcv)
    twin = (shot, run * 2 + 1 - core)
    up, down = (shot, rcv + 2), (shot, rcv - 2)

    barrier = pltpu.get_barrier_semaphore()
    for device in beside + [across, twin]:
        pl.semaphore_signal(barrier, inc=1, device_id=device, device_id_type=MESH)

    @pl.when(run < 3)
    def _():
        pl.semaphore_signal(barrier, inc=1, device_id=up, device_id_type=MESH)

    @pl.when(run > 0)
    def _():
        pl.semaphore_signal(barrier, inc=1, device_id=down, device_id_type=MESH)

    blocks = (block, LAST)
    ways = beside + [across]

    def piece(p, f, k):
        return rows.at[p, :, f, :, pl.ds(pl.multiple_of(k * LANES, LANES), LANES)]

    def copy(p, f, k, way):
        return pltpu.make_async_remote_copy(
            src_ref=piece(p, f, k), dst_ref=piece(p, f, k),
            send_sem=row_send.at[p, f, way], recv_sem=row_recv.at[p, f, k],
            device_id=ways[way], device_id_type=MESH,
        )

    streams = {}
    for p in range(2):
        sx, sy, sh = place_of(blocks[p])
        home = half == sh
        for f in range(NF):
            turn, other = f % 4, f // 4
            fx, fy = turned((x - sx + 4) % 4, (y - sy + 4) % 4, 4 - turn)
            place = fx * 4 + fy
            (edges, depth), (edges2, depth2) = HOME, AWAY[other]
            send = [None] * 5
            for way in range(4):
                send[(way + turn) % 4] = jnp.where(
                    home, bit(edges[way], place), bit(edges2[way], place)
                )
            gate = OTHER[other][0]
            send[4] = jnp.where(home & (place == gate[0] * 4 + gate[1]), 1, 0)
            late = sum(
                jnp.where(home, bit(depth[i], place), bit(depth2[i], place)) << i for i in range(4)
            )
            streams[p, f] = (send, late + other)

    def col_piece(p, i):
        return cols.at[p, :, pl.ds(i * (NF // COLS), NF // COLS)]

    def col_copy(p, i, way):
        return pltpu.make_async_remote_copy(
            src_ref=col_piece(p, i), dst_ref=col_piece(p, i),
            send_sem=col_send.at[p, way], recv_sem=col_recv.at[p, i],
            device_id=(up, down, twin)[way], device_id_type=MESH,
        )

    col_parts = {}
    for p in range(2):
        owner = blocks[p] // 4
        o_run, o_core = owner // 2, owner % 2
        mine = core == o_core
        goes_up = mine & (run >= o_run) & (run < 3)
        goes_down = mine & (run <= o_run) & (run > 0)
        far = jnp.abs(run - o_run)
        col_parts[p] = (mine, goes_up, goes_down, far)

    for p in range(2):
        owner = blocks[p] // 4
        offset = (blocks[p] % 4) * SIDE

        @pl.when(shot == blocks[p])
        def _(p=p):
            def one(k, _):
                for f in range(NF):
                    src = data.at[:, f, :, pl.ds(pl.multiple_of(k * LANES, LANES), LANES)]
                    pltpu.make_async_copy(src, piece(p, f, k), row_recv.at[p, f, k]).start()
                return 0
            lax.fori_loop(0, PIECES, one, 0)

        @pl.when(rcv == owner)
        def _(p=p, offset=offset):
            def one(i, _):
                src = data.at[:, pl.ds(i * (NF // COLS), NF // COLS), :, pl.ds(offset, SIDE)]
                pltpu.make_async_copy(src, col_piece(p, i), col_recv.at[p, i]).start()
                return 0
            lax.fori_loop(0, COLS, one, 0)

    inner = jnp.where((run > 0) & (run < 3), 1, 0)
    pl.semaphore_wait(barrier, 7 + inner)

    def step(s, _):
        for f in range(NF):
            for p in range(2):
                send, late = streams[p, f]
                left = s - late

                @pl.when((left >= 0) & (left < 2 * PIECES) & (left % 2 == 0))
                def _(p=p, f=f, send=send, left=left):
                    k = left // 2
                    copy(p, f, k, 0).wait_recv()
                    for way in range(5):
                        @pl.when(send[way] == 1)
                        def _(way=way):
                            copy(p, f, k, way).start()
        for p in range(2):
            mine, goes_up, goes_down, far = col_parts[p]
            i = s - 1 - far

            @pl.when(mine & (i >= 0) & (i < COLS))
            def _(p=p, i=i, goes_up=goes_up, goes_down=goes_down):
                col_copy(p, i, 0).wait_recv()
                for way, go in ((0, goes_up), (1, goes_down)):
                    @pl.when(go)
                    def _(way=way):
                        col_copy(p, i, way).start()
                col_copy(p, i, 2).start()
        return 0

    lax.fori_loop(0, 2 * PIECES + 9, step, 0)

    for p in range(2):
        mine, goes_up, goes_down, far = col_parts[p]

        def whole(way, p=p):
            return pltpu.make_async_remote_copy(
                src_ref=cols.at[p], dst_ref=cols.at[p],
                send_sem=col_send.at[p, way], recv_sem=col_recv.at[p, 0],
                device_id=twin, device_id_type=MESH,
            )

        @pl.when(jnp.logical_not(mine))
        def _(p=p):
            for i in range(COLS):
                col_copy(p, i, 2).wait_recv()

        for way, go in ((0, goes_up), (1, goes_down), (2, mine)):
            @pl.when(go)
            def _(way=way, whole=whole):
                whole(way).wait_send()
        for f in range(NF):
            for way in range(5):
                @pl.when(streams[p, f][0][way] == 1)
                def _(p=p, f=f, way=way):
                    pltpu.make_async_remote_copy(
                        src_ref=rows.at[p, :, f], dst_ref=rows.at[p, :, f],
                        send_sem=row_send.at[p, f, way], recv_sem=row_recv.at[p, f, 0],
                        device_id=ways[way], device_id_type=MESH,
                    ).wait_send()


def gather(block, data):
    hbm = pl.BlockSpec(memory_space=pl.ANY)
    return pl.pallas_call(
        functools.partial(gather_kernel, block),
        out_shape=(
            jax.ShapeDtypeStruct((2,) + data.shape, data.dtype),
            jax.ShapeDtypeStruct((2,) + data.shape[:3] + (SIDE,), data.dtype),
        ),
        in_specs=[hbm],
        out_specs=(hbm, hbm),
        scratch_shapes=[
            pltpu.SemaphoreType.DMA((2, NF, PIECES)),
            pltpu.SemaphoreType.DMA((2, NF, 5)),
            pltpu.SemaphoreType.DMA((2, COLS)),
            pltpu.SemaphoreType.DMA((2, 3)),
            pltpu.SemaphoreType.DMA,
        ],
        compiler_params=pltpu.CompilerParams(collective_id=block, has_side_effects=True),
        name="gather",
    )(data)


def transform(re, im):
    def c(n):
        return math.cos(math.pi * n / 8)

    def s(n):
        return math.sin(math.pi * n / 8)

    a = c(2)
    quarter = []
    for t in range(4):
        main = (re[4], -im[4], -re[4], im[4])[t]
        last = re[8] if t % 2 == 0 else -re[8]
        quarter.append(main + last - im[8] * s(8 * t))
    d, e = a * (re[2] - re[6]), a * (im[2] + im[6])
    anti = [re[2] + re[6], d - e, im[6] - im[2], -d - e]
    even = [quarter[t] + anti[t] for t in range(4)] + [quarter[t] - anti[t] for t in range(4)]
    p1, q1, p3, q3 = re[1] + re[7], im[1] - im[7], re[3] + re[5], im[3] - im[5]
    m1, n1, m3, n3 = re[1] - re[7], im[1] + im[7], re[3] - re[5], im[3] + im[5]
    g, h = a * (p1 - p3), a * (q1 + q3)
    u, v = c(1) * m1 + s(1) * m3, s(1) * n1 + c(1) * n3
    w, z = s(1) * m1 - c(1) * m3, c(1) * n1 - s(1) * n3
    odd = [p1 + p3, u - v, g - h, w - z, q3 - q1, -w - z, -g - h, -u - v]
    return [even[t] + odd[t] for t in range(8)] + [even[t] - odd[t] for t in range(8)]


def multiply_kernel(wave, rows, cols, out, left, product):
    @pl.when(pl.program_id(0) == 0)
    def _():
        for f in range(NF):
            for p in range(2):
                lr, li = cols[p, 0, f], cols[p, 1, f]
                left[f, :SIDE, 2 * p * SIDE:(2 * p + 1) * SIDE] = lr
                left[f, :SIDE, (2 * p + 1) * SIDE:(2 * p + 2) * SIDE] = -li
                left[f, SIDE:, 2 * p * SIDE:(2 * p + 1) * SIDE] = li
                left[f, SIDE:, (2 * p + 1) * SIDE:(2 * p + 2) * SIDE] = lr

    for f in range(NF):
        right = jnp.concatenate([rows[p, c, f] for p in range(2) for c in range(2)], axis=0)
        product[f] = jnp.dot(left[f], right, preferred_element_type=jnp.float32)

    high = 16
    def tile(i, _):
        at = pl.ds(pl.multiple_of(i * high, high), high)
        at2 = pl.ds(pl.multiple_of(i * high + SIDE, high), high)
        re, im = [None], [None]
        for f in range(NF):
            pr, pi = product[f, at, :], product[f, at2, :]
            wr, wi = wave[0, f], wave[1, f]
            re.append(wr * pr - wi * pi)
            im.append(wr * pi + wi * pr)
        for t, sample in enumerate(transform(re, im)):
            out[t, at, :] = sample.astype(out.dtype)
        return 0

    lax.fori_loop(0, SIDE // high, tile, 0)


def multiply(wave, rows, cols):
    width = rows.shape[-1]
    tile = 128
    return pl.pallas_call(
        multiply_kernel,
        grid=(width // tile,),
        out_shape=jax.ShapeDtypeStruct((2 * NF, SIDE, width), rows.dtype),
        in_specs=[
            pl.BlockSpec(memory_space=pltpu.SMEM),
            pl.BlockSpec((2, 2, NF, SIDE, tile), lambda i: (0, 0, 0, 0, i)),
            pl.BlockSpec((2, 2, NF, SIDE, SIDE), lambda i: (0, 0, 0, 0, 0)),
        ],
        out_specs=pl.BlockSpec((2 * NF, SIDE, tile), lambda i: (0, 0, i)),
        scratch_shapes=[
            pltpu.VMEM((NF, 2 * SIDE, 4 * SIDE), rows.dtype),
            pltpu.VMEM((NF, 2 * SIDE, tile), jnp.float32),
        ],
        compiler_params=pltpu.CompilerParams(vmem_limit_bytes=32 * 2**20),
        name="multiply",
    )(wave, rows, cols)


def shards(data, inverse_wavelet, panel_blocks):
    block = jnp.where(panel_blocks[0] == LAST, panel_blocks[1], panel_blocks[0])
    rows, cols = lax.switch(block, [functools.partial(gather, b) for b in range(LAST)], data)
    return multiply(inverse_wavelet * NF ** -0.5, rows, cols)


def solution(mesh):
    placed = (P(None, None, "shot", "rcv"), P(), P())
    return jax.shard_map(
        shards, mesh=mesh, in_specs=placed, out_specs=P(None, "shot", "rcv"), check_vma=False
    )
```

```python
import functools
import math

import jax
import jax.numpy as jnp
from jax import lax
from jax.experimental import pallas as pl
from jax.experimental.pallas import tpu as pltpu
from jax.sharding import PartitionSpec as P

MESH = pl.DeviceIdType.MESH
LAST = 31
NF, SIDE, LANES = 8, 128, 128
PARTS = 1
PIECES = 4 * PARTS
PIECE = (SIDE, LANES) if PARTS == 2 else (2, SIDE, LANES)
PERIOD = 2
COLS = 4
STEPS = ((1, 0), (0, 1), (-1, 0), (0, -1))

TREE = (
    (0, 0, 0), (1, 0, 1), (1, 0, 3), (1, 0, 0), (2, 0, 0), (1, 1, 2), (1, 1, 0), (1, 3, 2),
    (1, 1, 1), (2, 0, 3), (2, 3, 0), (1, 2, 2), (1, 2, 0), (2, 1, 0), (2, 2, 0),
)
OTHER = (
    ((1, 3), 2, (
        (1, 3, 0), (1, 3, 1), (1, 3, 3), (1, 3, 2), (0, 3, 1), (0, 3, 2), (1, 2, 0), (1, 2, 2),
        (1, 2, 3), (2, 3, 1), (0, 2, 2), (0, 0, 2), (2, 2, 3), (0, 2, 3), (3, 2, 3),
    )),
    ((1, 0), 1, (
        (1, 0, 0), (1, 0, 3), (1, 0, 1), (1, 0, 2), (1, 3, 2), (1, 1, 2), (1, 3, 0), (1, 3, 3),
        (2, 0, 1), (0, 0, 2), (0, 1, 2), (0, 3, 3), (2, 3, 3), (2, 3, 0), (2, 2, 0),
    )),
)
SKEW = 2
CROSS = 2


def tables(root, edges, base):
    depth = {root: base}
    while len(depth) < 16:
        for x, y, d in edges:
            if (x, y) in depth:
                there = ((x + STEPS[d][0]) % 4, (y + STEPS[d][1]) % 4)
                depth.setdefault(there, depth[(x, y)] + 1)
    masks = [sum(1 << (x * 4 + y) for x, y, d in edges if d == way) for way in range(4)]
    bits = [
        sum(1 << (x * 4 + y) for (x, y), v in depth.items() if (v >> i) & 1) for i in range(4)
    ]
    return masks, bits


HOME = tables((0, 0), TREE, 0)
AWAY = [tables(root, edges, base + CROSS) for root, base, edges in OTHER]
GATES = [root[0] * 4 + root[1] for root, base, edges in OTHER]


def place_of(block):
    return block % 4, block // 8, (block // 4) % 2


def bit(mask, place):
    return (mask >> place) & 1


def gather_kernel(block, data, rows, cols, table, row_recv, row_send, col_recv, col_send):
    shot, rcv = lax.axis_index("shot"), lax.axis_index("rcv")
    x, half, y = shot % 4, (shot // 4) % 2, shot // 8
    run, core = rcv // 2, rcv % 2

    def at(px, py, ph):
        return (py * 2 + ph) * 4 + px

    beside = [(at((x + a + 4) % 4, (y + b + 4) % 4, half), rcv) for a, b in STEPS]
    ways = beside + [(at(x, y, 1 - half), rcv)]
    col_ways = [(shot, rcv + 2), (shot, rcv - 2), (shot, run * 2 + 1 - core)]

    barrier = pltpu.get_barrier_semaphore()
    for device in ways + [col_ways[2]]:
        pl.semaphore_signal(barrier, inc=1, device_id=device, device_id_type=MESH)

    @pl.when(run < 3)
    def _():
        pl.semaphore_signal(barrier, inc=1, device_id=col_ways[0], device_id_type=MESH)

    @pl.when(run > 0)
    def _():
        pl.semaphore_signal(barrier, inc=1, device_id=col_ways[1], device_id_type=MESH)

    def either(p, values):
        return jnp.where(p == 0, values[0], values[1])

    blocks = (block, LAST)
    places = [place_of(b) for b in blocks]

    def piece(p, f, k):
        return rows.at[p, f, k]

    def copy(p, f, k, way):
        return pltpu.make_async_remote_copy(
            src_ref=piece(p, f, k), dst_ref=piece(p, f, k),
            send_sem=row_send.at[p, f, way], recv_sem=row_recv.at[p, f, k],
            device_id=ways[way], device_id_type=MESH,
        )

    per_col = NF // COLS

    def col_piece(p, i):
        return cols.at[p, :, pl.ds(i * per_col, per_col)]

    def col_copy(p, i, way):
        return pltpu.make_async_remote_copy(
            src_ref=col_piece(p, i), dst_ref=col_piece(p, i),
            send_sem=col_send.at[p, way], recv_sem=col_recv.at[p, i],
            device_id=col_ways[way], device_id_type=MESH,
        )

    def col_part(p):
        owner = either(p, [b // 4 for b in blocks])
        far = jnp.abs(run - owner // 2)
        mine = core == owner % 2
        goes_up = mine & (run >= owner // 2) & (run < 3)
        goes_down = mine & (run <= owner // 2) & (run > 0)
        return far, (goes_up, goes_down, mine)

    def own(p, _):
        @pl.when(shot == either(p, blocks))
        def _():
            def one(n, _):
                k, f = n // NF, n % NF
                lanes = pl.ds(pl.multiple_of((k // PARTS) * LANES, LANES), LANES)
                src = data.at[k % 2, f, :, lanes] if PARTS == 2 else data.at[:, f, :, lanes]
                pltpu.make_async_copy(src, piece(p, f, k), row_recv.at[p, f, k]).start()
                return 0
            lax.fori_loop(0, PIECES * NF, one, 0)

        @pl.when(rcv == either(p, [b // 4 for b in blocks]))
        def _():
            offset = either(p, [(b % 4) * SIDE for b in blocks])
            lanes = pl.ds(pl.multiple_of(offset, SIDE), SIDE)

            def one(i, _):
                src = data.at[:, pl.ds(i * per_col, per_col), :, lanes]
                pltpu.make_async_copy(src, col_piece(p, i), col_recv.at[p, i]).start()
                return 0
            lax.fori_loop(0, COLS, one, 0)
        return 0

    lax.fori_loop(0, 2, own, 0)

    def plan(n, _):
        f, p = n // 2, n % 2
        sx, sy, sh = (either(p, [place[i] for place in places]) for i in range(3))
        home = half == sh
        turn, other = f % 4, f // 4
        rx, ry = (x - sx + 4) % 4, (y - sy + 4) % 4
        nx, ny = (4 - rx) % 4, (4 - ry) % 4

        def turned(a, b, c, d):
            return jnp.where(turn == 0, a, jnp.where(turn == 1, b, jnp.where(turn == 2, c, d)))

        place = turned(rx, ry, nx, ny) * 4 + turned(ry, nx, ny, rx)

        def pick(part, i):
            away = jnp.where(other == 0, AWAY[0][part][i], AWAY[1][part][i])
            return bit(jnp.where(home, HOME[part][i], away), place)

        word = 0
        for way in range(4):
            word = word + (pick(0, way) << ((way + turn) % 4))
        gate = jnp.where(other == 0, GATES[0], GATES[1])
        word = word + jnp.where(home & (place == gate), 16, 0)
        late = SKEW * sum(pick(1, i) << i for i in range(4)) + other * (PERIOD // 2)
        table[n] = late * 32 + word
        return 0

    lax.fori_loop(0, 2 * NF, plan, 0)
    inner = jnp.where((run > 0) & (run < 3), 1, 0)
    pl.semaphore_wait(barrier, 7 + inner)

    def step(s, _):
        def stream(n, _):
            f, p = n // 2, n % 2
            word = table[n]
            left = s - word // 32

            @pl.when((left >= 0) & (left < PERIOD * PIECES) & (left % PERIOD == 0))
            def _():
                k = left // PERIOD
                copy(p, f, k, 0).wait_recv()
                for way in range(5):
                    @pl.when((word // 2**way) % 2 == 1)
                    def _(way=way):
                        copy(p, f, k, way).start()
            return 0

        lax.fori_loop(0, 2 * NF, stream, 0)

        def column(p, _):
            far, goes = col_part(p)
            i = s - 1 - 2 * far

            @pl.when(goes[2] & (i >= 0) & (i < COLS))
            def _():
                col_copy(p, i, 2).wait_recv()
                for way in range(3):
                    @pl.when(goes[way])
                    def _(way=way):
                        col_copy(p, i, way).start()
            return 0

        lax.fori_loop(0, 2, column, 0)
        return 0

    lax.fori_loop(0, PERIOD * PIECES + 8 * SKEW, step, 0)

    def rest(p, _):
        goes = col_part(p)[1]

        @pl.when(jnp.logical_not(goes[2]))
        def _():
            def one(i, _):
                col_copy(p, i, 2).wait_recv()
                return 0
            lax.fori_loop(0, COLS, one, 0)

        for way in range(3):
            @pl.when(goes[way])
            def _(way=way):
                pltpu.make_async_remote_copy(
                    src_ref=cols.at[p], dst_ref=cols.at[p],
                    send_sem=col_send.at[p, way], recv_sem=col_recv.at[p, 0],
                    device_id=col_ways[2], device_id_type=MESH,
                ).wait_send()
        return 0

    lax.fori_loop(0, 2, rest, 0)

    def sent(n, _):
        f, p = n // 2, n % 2
        word = table[n]
        for way in range(5):
            @pl.when((word // 2**way) % 2 == 1)
            def _(way=way):
                pltpu.make_async_remote_copy(
                    src_ref=rows.at[p, f], dst_ref=rows.at[p, f],
                    send_sem=row_send.at[p, f, way], recv_sem=row_recv.at[p, f, 0],
                    device_id=ways[way], device_id_type=MESH,
                ).wait_send()
        return 0

    lax.fori_loop(0, 2 * NF, sent, 0)


def gather(block, data):
    vmem = pl.BlockSpec(memory_space=pltpu.VMEM)
    return pl.pallas_call(
        functools.partial(gather_kernel, block),
        out_shape=(
            jax.ShapeDtypeStruct((2, NF, PIECES) + PIECE, data.dtype),
            jax.ShapeDtypeStruct((2,) + data.shape[:3] + (SIDE,), data.dtype),
        ),
        in_specs=[pl.BlockSpec(memory_space=pltpu.HBM)],
        out_specs=(vmem, vmem),
        scratch_shapes=[
            pltpu.SMEM((2 * NF,), jnp.int32),
            pltpu.SemaphoreType.DMA((2, NF, PIECES)),
            pltpu.SemaphoreType.DMA((2, NF, 5)),
            pltpu.SemaphoreType.DMA((2, COLS)),
            pltpu.SemaphoreType.DMA((2, 3)),
        ],
        compiler_params=pltpu.CompilerParams(
            collective_id=block, has_side_effects=True, vmem_limit_bytes=16 * 2**20
        ),
        name="gather",
    )(data)


def transform(re, im):
    def c(n):
        return math.cos(math.pi * n / 8)

    def s(n):
        return math.sin(math.pi * n / 8)

    a = c(2)
    quarter = []
    for t in range(4):
        main = (re[4], -im[4], -re[4], im[4])[t]
        last = re[8] if t % 2 == 0 else -re[8]
        quarter.append(main + last - im[8] * s(8 * t))
    d, e = a * (re[2] - re[6]), a * (im[2] + im[6])
    anti = [re[2] + re[6], d - e, im[6] - im[2], -d - e]
    even = [quarter[t] + anti[t] for t in range(4)] + [quarter[t] - anti[t] for t in range(4)]
    p1, q1, p3, q3 = re[1] + re[7], im[1] - im[7], re[3] + re[5], im[3] - im[5]
    m1, n1, m3, n3 = re[1] - re[7], im[1] + im[7], re[3] - re[5], im[3] + im[5]
    g, h = a * (p1 - p3), a * (q1 + q3)
    u, v = c(1) * m1 + s(1) * m3, s(1) * n1 + c(1) * n3
    w, z = s(1) * m1 - c(1) * m3, c(1) * n1 - s(1) * n3
    odd = [p1 + p3, u - v, g - h, w - z, q3 - q1, -w - z, -g - h, -u - v]
    return [even[t] + odd[t] for t in range(8)] + [even[t] - odd[t] for t in range(8)]


def multiply_kernel(wave, rows, cols, out, left, product):
    @pl.when(pl.program_id(0) == 0)
    def _():
        for f in range(NF):
            for p in range(2):
                lr, li = cols[p, 0, f], cols[p, 1, f]
                left[f, :SIDE, 2 * p * SIDE:(2 * p + 1) * SIDE] = lr
                left[f, :SIDE, (2 * p + 1) * SIDE:(2 * p + 2) * SIDE] = -li
                left[f, SIDE:, 2 * p * SIDE:(2 * p + 1) * SIDE] = li
                left[f, SIDE:, (2 * p + 1) * SIDE:(2 * p + 2) * SIDE] = lr

    for f in range(NF):
        right = jnp.concatenate([rows[p, f, c] if PARTS == 2 else rows[p, f, 0, c] for p in range(2) for c in range(2)], axis=0)
        product[f] = jnp.dot(left[f], right, preferred_element_type=jnp.float32)

    high = 16
    def tile(i, _):
        at = pl.ds(pl.multiple_of(i * high, high), high)
        at2 = pl.ds(pl.multiple_of(i * high + SIDE, high), high)
        re, im = [None], [None]
        for f in range(NF):
            pr, pi = product[f, at, :], product[f, at2, :]
            wr, wi = wave[0, f], wave[1, f]
            re.append(wr * pr - wi * pi)
            im.append(wr * pi + wi * pr)
        for t, sample in enumerate(transform(re, im)):
            out[t, at, :] = sample.astype(out.dtype)
        return 0

    lax.fori_loop(0, SIDE // high, tile, 0)


def multiply(wave, rows, cols):
    tile = LANES
    width = PIECES // PARTS * tile
    return pl.pallas_call(
        multiply_kernel,
        grid=(width // tile,),
        out_shape=jax.ShapeDtypeStruct((2 * NF, SIDE, width), rows.dtype),
        in_specs=[
            pl.BlockSpec(memory_space=pltpu.SMEM),
            pl.BlockSpec((2, NF, PARTS) + PIECE, lambda i: (0, 0, i) + (0,) * len(PIECE)),
            pl.BlockSpec((2, 2, NF, SIDE, SIDE), lambda i: (0, 0, 0, 0, 0)),
        ],
        out_specs=pl.BlockSpec((2 * NF, SIDE, tile), lambda i: (0, 0, i)),
        scratch_shapes=[
            pltpu.VMEM((NF, 2 * SIDE, 4 * SIDE), rows.dtype),
            pltpu.VMEM((NF, 2 * SIDE, tile), jnp.float32),
        ],
        compiler_params=pltpu.CompilerParams(vmem_limit_bytes=32 * 2**20),
        name="multiply",
    )(wave, rows, cols)


def shards(data, inverse_wavelet, panel_blocks):
    block = jnp.where(panel_blocks[0] == LAST, panel_blocks[1], panel_blocks[0])
    rows, cols = lax.switch(block, [functools.partial(gather, b) for b in range(LAST)], data)
    return multiply(inverse_wavelet * NF ** -0.5, rows, cols)


def solution(mesh):
    placed = (P(None, None, "shot", "rcv"), P(), P())
    return jax.shard_map(
        shards, mesh=mesh, in_specs=placed, out_specs=P(None, "shot", "rcv"), check_vma=False
    )
```

```python
import functools
import math

import jax
import jax.numpy as jnp
from jax import lax
from jax.experimental import pallas as pl
from jax.experimental.pallas import tpu as pltpu
from jax.sharding import PartitionSpec as P

MESH = pl.DeviceIdType.MESH
LAST = 31
NF, SIDE, LANES = 8, 128, 128
PIECES = 4
PIECE = (2, SIDE, LANES)
TILES = 2
SHIFT = 1
PERIOD = 1 << SHIFT
COLS = 4
STEPS = ((1, 0), (0, 1), (-1, 0), (0, -1))

TREE = (
    (0, 0, 0), (1, 0, 1), (1, 0, 3), (1, 0, 0), (2, 0, 0), (1, 1, 2), (1, 1, 0), (1, 3, 2),
    (1, 1, 1), (2, 0, 3), (2, 3, 0), (1, 2, 2), (1, 2, 0), (2, 1, 0), (2, 2, 0),
)
OTHER = (
    ((1, 3), 2, (
        (1, 3, 0), (1, 3, 1), (1, 3, 3), (1, 3, 2), (0, 3, 1), (0, 3, 2), (1, 2, 0), (1, 2, 2),
        (1, 2, 3), (2, 3, 1), (0, 2, 2), (0, 0, 2), (2, 2, 3), (0, 2, 3), (3, 2, 3),
    )),
    ((1, 0), 1, (
        (1, 0, 0), (1, 0, 3), (1, 0, 1), (1, 0, 2), (1, 3, 2), (1, 1, 2), (1, 3, 0), (1, 3, 3),
        (2, 0, 1), (0, 0, 2), (0, 1, 2), (0, 3, 3), (2, 3, 3), (2, 3, 0), (2, 2, 0),
    )),
)
SKEW = 2
CROSS = 2


def tables(root, edges, base):
    depth = {root: base}
    while len(depth) < 16:
        for x, y, d in edges:
            if (x, y) in depth:
                there = ((x + STEPS[d][0]) % 4, (y + STEPS[d][1]) % 4)
                depth.setdefault(there, depth[(x, y)] + 1)
    masks = [sum(1 << (x * 4 + y) for x, y, d in edges if d == way) for way in range(4)]
    bits = [
        sum(1 << (x * 4 + y) for (x, y), v in depth.items() if (v >> i) & 1) for i in range(4)
    ]
    return masks, bits


HOME = tables((0, 0), TREE, 0)
AWAY = [tables(root, edges, base + CROSS) for root, base, edges in OTHER]
GATES = [root[0] * 4 + root[1] for root, base, edges in OTHER]


def place_of(block):
    return block % 4, block // 8, (block // 4) % 2


def bit(mask, place):
    return (mask >> place) & 1


def gather_kernel(block, data, rows_hbm, cols, rows, lates, words, out_sem, row_recv, row_send, col_recv, col_send):
    shot, rcv = lax.axis_index("shot"), lax.axis_index("rcv")
    x, half, y = shot & 3, (shot >> 2) & 1, shot >> 3
    run, core = rcv >> 1, rcv & 1

    def at(px, py, ph):
        return (py * 2 + ph) * 4 + px

    beside = [(at((x + a) & 3, (y + b) & 3, half), rcv) for a, b in STEPS]
    ways = beside + [(at(x, y, 1 - half), rcv)]
    col_ways = [(shot, rcv + 2), (shot, rcv - 2), (shot, run * 2 + 1 - core)]

    barrier = pltpu.get_barrier_semaphore()
    for device in ways + [col_ways[2]]:
        pl.semaphore_signal(barrier, inc=1, device_id=device, device_id_type=MESH)

    @pl.when(run < 3)
    def _():
        pl.semaphore_signal(barrier, inc=1, device_id=col_ways[0], device_id_type=MESH)

    @pl.when(run > 0)
    def _():
        pl.semaphore_signal(barrier, inc=1, device_id=col_ways[1], device_id_type=MESH)

    def either(p, values):
        return jnp.where(p == 0, values[0], values[1])

    blocks = (block, LAST)
    places = [place_of(b) for b in blocks]

    def piece(p, f, k):
        return rows.at[p, f, k]

    def copy(p, f, k, way):
        return pltpu.make_async_remote_copy(
            src_ref=piece(p, f, k), dst_ref=piece(p, f, k),
            send_sem=row_send.at[p, f, way], recv_sem=row_recv.at[p, f, k],
            device_id=ways[way], device_id_type=MESH,
        )

    per_col = NF // COLS

    def col_piece(p, i):
        return cols.at[p, :, pl.ds(i * per_col, per_col)]

    def col_copy(p, i, way):
        return pltpu.make_async_remote_copy(
            src_ref=col_piece(p, i), dst_ref=col_piece(p, i),
            send_sem=col_send.at[p, way], recv_sem=col_recv.at[p, i],
            device_id=col_ways[way], device_id_type=MESH,
        )

    def col_part(p):
        owner = either(p, [b // 4 for b in blocks])
        o_run = owner >> 1
        far = jnp.abs(run - o_run)
        mine = core == (owner & 1)
        goes_up = mine & (run >= o_run) & (run < 3)
        goes_down = mine & (run <= o_run) & (run > 0)
        return far, (goes_up, goes_down, mine)

    def own(p, _):
        @pl.when(shot == either(p, blocks))
        def _():
            def one(n, _):
                k, f = n >> 3, n & 7
                lanes = pl.ds(pl.multiple_of(k * LANES, LANES), LANES)
                src = data.at[:, f, :, lanes]
                pltpu.make_async_copy(src, piece(p, f, k), row_recv.at[p, f, k]).start()
                return 0
            lax.fori_loop(0, PIECES * NF, one, 0)

        @pl.when(rcv == either(p, [b // 4 for b in blocks]))
        def _():
            offset = either(p, [(b % 4) * SIDE for b in blocks])
            lanes = pl.ds(pl.multiple_of(offset, SIDE), SIDE)

            def one(i, _):
                src = data.at[:, pl.ds(i * per_col, per_col), :, lanes]
                pltpu.make_async_copy(src, col_piece(p, i), col_recv.at[p, i]).start()
                return 0
            lax.fori_loop(0, COLS, one, 0)
        return 0

    lax.fori_loop(0, 2, own, 0)

    def plan(n, _):
        f, p = n >> 1, n & 1
        sx, sy, sh = (either(p, [place[i] for place in places]) for i in range(3))
        home = half == sh
        turn, other = f & 3, f >> 2
        rx, ry = (x - sx) & 3, (y - sy) & 3
        nx, ny = -rx & 3, -ry & 3

        def turned(a, b, c, d):
            return jnp.where(turn == 0, a, jnp.where(turn == 1, b, jnp.where(turn == 2, c, d)))

        place = turned(rx, ry, nx, ny) * 4 + turned(ry, nx, ny, rx)

        def pick(part, i):
            away = jnp.where(other == 0, AWAY[0][part][i], AWAY[1][part][i])
            return bit(jnp.where(home, HOME[part][i], away), place)

        word = 0
        for way in range(4):
            word = word + (pick(0, way) << ((way + turn) & 3))
        gate = jnp.where(other == 0, GATES[0], GATES[1])
        word = word + jnp.where(home & (place == gate), 16, 0)
        late = SKEW * sum(pick(1, i) << i for i in range(4)) + other * (PERIOD // 2)
        lates[n] = late
        words[n] = word
        return 0

    lax.fori_loop(0, 2 * NF, plan, 0)
    inner = jnp.where((run > 0) & (run < 3), 1, 0)
    pl.semaphore_wait(barrier, 7 + inner)

    def step(s, _):
        def stream(n, _):
            left = s - lates[n]

            @pl.when((left & ~(PERIOD * (PIECES - 1))) == 0)
            def _():
                f, p = n >> 1, n & 1
                k = left >> SHIFT
                word = words[n]
                copy(p, f, k, 0).wait_recv()
                pltpu.make_async_copy(piece(p, f, k), rows_hbm.at[p, f, k], out_sem).start()
                for way in range(5):
                    @pl.when((word & (1 << way)) != 0)
                    def _(way=way):
                        copy(p, f, k, way).start()
            return 0

        lax.fori_loop(0, 2 * NF, stream, 0)

        def column(p, _):
            far, goes = col_part(p)
            i = s - 1 - 4 * far

            @pl.when(goes[2] & (i >= 0) & (i < COLS))
            def _():
                col_copy(p, i, 2).wait_recv()
                for way in range(3):
                    @pl.when(goes[way])
                    def _(way=way):
                        col_copy(p, i, way).start()
            return 0

        lax.fori_loop(0, 2, column, 0)
        return 0

    lax.fori_loop(0, PERIOD * PIECES + 8 * SKEW, step, 0)

    pltpu.make_async_copy(rows, rows_hbm, out_sem).wait()
    def rest(p, _):
        goes = col_part(p)[1]

        @pl.when(jnp.logical_not(goes[2]))
        def _():
            def one(i, _):
                col_copy(p, i, 2).wait_recv()
                return 0
            lax.fori_loop(0, COLS, one, 0)

        for way in range(3):
            @pl.when(goes[way])
            def _(way=way):
                pltpu.make_async_remote_copy(
                    src_ref=cols.at[p], dst_ref=cols.at[p],
                    send_sem=col_send.at[p, way], recv_sem=col_recv.at[p, 0],
                    device_id=col_ways[2], device_id_type=MESH,
                ).wait_send()
        return 0

    lax.fori_loop(0, 2, rest, 0)

    def sent(n, _):
        f, p = n >> 1, n & 1
        word = words[n]
        for way in range(5):
            @pl.when((word & (1 << way)) != 0)
            def _(way=way):
                pltpu.make_async_remote_copy(
                    src_ref=rows.at[p, f], dst_ref=rows.at[p, f],
                    send_sem=row_send.at[p, f, way], recv_sem=row_recv.at[p, f, 0],
                    device_id=ways[way], device_id_type=MESH,
                ).wait_send()
        return 0

    lax.fori_loop(0, 2 * NF, sent, 0)


def gather(block, data):
    vmem, hbm = (pl.BlockSpec(memory_space=m) for m in (pltpu.VMEM, pltpu.HBM))
    landing = (2, NF, PIECES) + PIECE
    return pl.pallas_call(
        functools.partial(gather_kernel, block),
        out_shape=(
            jax.ShapeDtypeStruct(landing, data.dtype),
            jax.ShapeDtypeStruct((2,) + data.shape[:3] + (SIDE,), data.dtype),
        ),
        in_specs=[hbm],
        out_specs=(hbm, vmem),
        scratch_shapes=[
            pltpu.VMEM(landing, data.dtype),
            pltpu.SMEM((2 * NF,), jnp.int32),
            pltpu.SMEM((2 * NF,), jnp.int32),
            pltpu.SemaphoreType.DMA,
            pltpu.SemaphoreType.DMA((2, NF, PIECES)),
            pltpu.SemaphoreType.DMA((2, NF, 5)),
            pltpu.SemaphoreType.DMA((2, COLS)),
            pltpu.SemaphoreType.DMA((2, 3)),
        ],
        compiler_params=pltpu.CompilerParams(
            collective_id=block, has_side_effects=True, vmem_limit_bytes=16 * 2**20
        ),
        name="gather",
    )(data)


def transform(re, im):
    def c(n):
        return math.cos(math.pi * n / 8)

    def s(n):
        return math.sin(math.pi * n / 8)

    a = c(2)
    quarter = []
    for t in range(4):
        main = (re[4], -im[4], -re[4], im[4])[t]
        last = re[8] if t % 2 == 0 else -re[8]
        quarter.append(main + last - im[8] * s(8 * t))
    d, e = a * (re[2] - re[6]), a * (im[2] + im[6])
    anti = [re[2] + re[6], d - e, im[6] - im[2], -d - e]
    even = [quarter[t] + anti[t] for t in range(4)] + [quarter[t] - anti[t] for t in range(4)]
    p1, q1, p3, q3 = re[1] + re[7], im[1] - im[7], re[3] + re[5], im[3] - im[5]
    m1, n1, m3, n3 = re[1] - re[7], im[1] + im[7], re[3] - re[5], im[3] + im[5]
    g, h = a * (p1 - p3), a * (q1 + q3)
    u, v = c(1) * m1 + s(1) * m3, s(1) * n1 + c(1) * n3
    w, z = s(1) * m1 - c(1) * m3, c(1) * n1 - s(1) * n3
    odd = [p1 + p3, u - v, g - h, w - z, q3 - q1, -w - z, -g - h, -u - v]
    return [even[t] + odd[t] for t in range(8)] + [even[t] - odd[t] for t in range(8)]


def multiply_kernel(wave, rows_hbm, cols, out, rows, left, product, staged, load_sem, sem):
    loads = []
    for i in range(PIECES // TILES):
        some = pl.ds(i * TILES, TILES)
        loads.append(
            pltpu.make_async_copy(rows_hbm.at[:, :, some], rows.at[:, :, some], load_sem.at[i])
        )
        loads[i].start()

    for f in range(NF):
        for p in range(2):
            lr, li = cols[p, 0, f], cols[p, 1, f]
            left[f, :SIDE, 2 * p * SIDE:(2 * p + 1) * SIDE] = lr
            left[f, :SIDE, (2 * p + 1) * SIDE:(2 * p + 2) * SIDE] = -li
            left[f, SIDE:, 2 * p * SIDE:(2 * p + 1) * SIDE] = li
            left[f, SIDE:, (2 * p + 1) * SIDE:(2 * p + 2) * SIDE] = lr

    width = TILES * LANES
    copies = []
    for i in range(PIECES // TILES):
        loads[i].wait()
        for f in range(NF):
            right = jnp.concatenate(
                [
                    jnp.concatenate([rows[p, f, i * TILES + j, c] for j in range(TILES)], axis=1)
                    for p in range(2)
                    for c in range(2)
                ],
                axis=0,
            )
            product[f] = jnp.dot(left[f], right, preferred_element_type=jnp.float32)

        high = 16

        def tile(h, _, i=i):
            at = pl.ds(pl.multiple_of(h * high, high), high)
            at2 = pl.ds(pl.multiple_of(h * high + SIDE, high), high)
            re, im = [None], [None]
            for f in range(NF):
                pr, pi = product[f, at, :], product[f, at2, :]
                wr, wi = wave[0, f] * NF ** -0.5, wave[1, f] * NF ** -0.5
                re.append(wr * pr - wi * pi)
                im.append(wr * pi + wi * pr)
            for t, sample in enumerate(transform(re, im)):
                staged[i, t, at, :] = sample.astype(staged.dtype)
            return 0

        lax.fori_loop(0, SIDE // high, tile, 0)
        copies.append(
            pltpu.make_async_copy(
                staged.at[i], out.at[:, :, pl.ds(i * width, width)], sem.at[i]
            )
        )
        copies[i].start()
    for copy in copies:
        copy.wait()


def multiply(wave, rows, cols):
    width = TILES * LANES
    vmem, hbm = (pl.BlockSpec(memory_space=m) for m in (pltpu.VMEM, pltpu.HBM))
    return pl.pallas_call(
        multiply_kernel,
        out_shape=jax.ShapeDtypeStruct((2 * NF, SIDE, PIECES * LANES), rows.dtype),
        in_specs=[pl.BlockSpec(memory_space=pltpu.SMEM), hbm, vmem],
        out_specs=hbm,
        scratch_shapes=[
            pltpu.VMEM(rows.shape, rows.dtype),
            pltpu.VMEM((NF, 2 * SIDE, 4 * SIDE), rows.dtype),
            pltpu.VMEM((NF, 2 * SIDE, width), jnp.float32),
            pltpu.VMEM((PIECES // TILES, 2 * NF, SIDE, width), rows.dtype),
            pltpu.SemaphoreType.DMA((PIECES // TILES,)),
            pltpu.SemaphoreType.DMA((PIECES // TILES,)),
        ],
        compiler_params=pltpu.CompilerParams(vmem_limit_bytes=24 * 2**20),
        name="multiply",
    )(wave, rows, cols)


def shards(data, inverse_wavelet, panel_blocks):
    block = jnp.min(panel_blocks)
    rows, cols = lax.switch(block, [functools.partial(gather, b) for b in range(LAST)], data)
    return multiply(inverse_wavelet, rows, cols)


def solution(mesh):
    placed = (P(None, None, "shot", "rcv"), P(), P())
    return jax.shard_map(
        shards, mesh=mesh, in_specs=placed, out_specs=P(None, "shot", "rcv"), check_vma=False
    )
```

```python
import functools
import math

import jax
import jax.numpy as jnp
from jax import lax
from jax.experimental import pallas as pl
from jax.experimental.pallas import tpu as pltpu
from jax.sharding import PartitionSpec as P

MESH = pl.DeviceIdType.MESH
LAST = 31
NF, SIDE, LANES = 8, 128, 128
PIECES = 4
PIECE = (2, SIDE, LANES)
TILES = 2
COLS = 4
STEPS = ((1, 0), (0, 1), (-1, 0), (0, -1))

TREE = (
    (0, 0, 0), (1, 0, 1), (1, 0, 3), (1, 0, 0), (2, 0, 0), (1, 1, 2), (1, 1, 0), (1, 3, 2),
    (1, 1, 1), (2, 0, 3), (2, 3, 0), (1, 2, 2), (1, 2, 0), (2, 1, 0), (2, 2, 0),
)
OTHER = (
    ((1, 3), 2, (
        (1, 3, 0), (1, 3, 1), (1, 3, 3), (1, 3, 2), (0, 3, 1), (0, 3, 2), (1, 2, 0), (1, 2, 2),
        (1, 2, 3), (2, 3, 1), (0, 2, 2), (0, 0, 2), (2, 2, 3), (0, 2, 3), (3, 2, 3),
    )),
    ((1, 0), 1, (
        (1, 0, 0), (1, 0, 3), (1, 0, 1), (1, 0, 2), (1, 3, 2), (1, 1, 2), (1, 3, 0), (1, 3, 3),
        (2, 0, 1), (0, 0, 2), (0, 1, 2), (0, 3, 3), (2, 3, 3), (2, 3, 0), (2, 2, 0),
    )),
)
SKEW = 2
CROSS = 2


def tables(root, edges, base):
    depth = {root: base}
    while len(depth) < 16:
        for x, y, d in edges:
            if (x, y) in depth:
                there = ((x + STEPS[d][0]) % 4, (y + STEPS[d][1]) % 4)
                depth.setdefault(there, depth[(x, y)] + 1)
    masks = [sum(1 << (x * 4 + y) for x, y, d in edges if d == way) for way in range(4)]
    bits = [
        sum(1 << (x * 4 + y) for (x, y), v in depth.items() if (v >> i) & 1) for i in range(4)
    ]
    return masks, bits


HOME = tables((0, 0), TREE, 0)
AWAY = [tables(root, edges, base + CROSS) for root, base, edges in OTHER]
GATES = [root[0] * 4 + root[1] for root, base, edges in OTHER]


def place_of(block):
    return block % 4, block // 8, (block // 4) % 2


def bit(mask, place):
    return (mask >> place) & 1


def gather_kernel(block, data, rows_hbm, cols, rows, lates, words, out_sem, row_recv, row_send, col_recv, col_send):
    shot, rcv = lax.axis_index("shot"), lax.axis_index("rcv")
    x, half, y = shot & 3, (shot >> 2) & 1, shot >> 3
    run, core = rcv >> 1, rcv & 1

    def at(px, py, ph):
        return (py * 2 + ph) * 4 + px

    beside = [(at((x + a) & 3, (y + b) & 3, half), rcv) for a, b in STEPS]
    ways = beside + [(at(x, y, 1 - half), rcv)]
    col_ways = [(shot, rcv + 2), (shot, rcv - 2), (shot, run * 2 + 1 - core)]

    barrier = pltpu.get_barrier_semaphore()
    for device in ways + [col_ways[2]]:
        pl.semaphore_signal(barrier, inc=1, device_id=device, device_id_type=MESH)

    @pl.when(run < 3)
    def _():
        pl.semaphore_signal(barrier, inc=1, device_id=col_ways[0], device_id_type=MESH)

    @pl.when(run > 0)
    def _():
        pl.semaphore_signal(barrier, inc=1, device_id=col_ways[1], device_id_type=MESH)

    def either(p, values):
        return jnp.where(p == 0, values[0], values[1])

    blocks = (block, LAST)
    places = [place_of(b) for b in blocks]
    shift = 1 if places[0][2] == places[1][2] else 0
    period = 1 << shift

    def piece(p, f, k):
        return rows.at[p, f, k]

    def copy(p, f, k, way):
        return pltpu.make_async_remote_copy(
            src_ref=piece(p, f, k), dst_ref=piece(p, f, k),
            send_sem=row_send.at[p, f, way], recv_sem=row_recv.at[p, f, k],
            device_id=ways[way], device_id_type=MESH,
        )

    per_col = NF // COLS

    def col_piece(p, i):
        return cols.at[p, :, pl.ds(i * per_col, per_col)]

    def col_copy(p, i, way):
        return pltpu.make_async_remote_copy(
            src_ref=col_piece(p, i), dst_ref=col_piece(p, i),
            send_sem=col_send.at[p, way], recv_sem=col_recv.at[p, i],
            device_id=col_ways[way], device_id_type=MESH,
        )

    def col_part(p):
        owner = either(p, [b // 4 for b in blocks])
        o_run = owner >> 1
        far = jnp.abs(run - o_run)
        mine = core == (owner & 1)
        goes_up = mine & (run >= o_run) & (run < 3)
        goes_down = mine & (run <= o_run) & (run > 0)
        return far, (goes_up, goes_down, mine)

    def own(p, _):
        @pl.when(shot == either(p, blocks))
        def _():
            def one(n, _):
                k, f = n >> 3, n & 7
                lanes = pl.ds(pl.multiple_of(k * LANES, LANES), LANES)
                src = data.at[:, f, :, lanes]
                pltpu.make_async_copy(src, piece(p, f, k), row_recv.at[p, f, k]).start()
                return 0
            lax.fori_loop(0, PIECES * NF, one, 0)

        @pl.when(rcv == either(p, [b // 4 for b in blocks]))
        def _():
            offset = either(p, [(b % 4) * SIDE for b in blocks])
            lanes = pl.ds(pl.multiple_of(offset, SIDE), SIDE)

            def one(i, _):
                src = data.at[:, pl.ds(i * per_col, per_col), :, lanes]
                pltpu.make_async_copy(src, col_piece(p, i), col_recv.at[p, i]).start()
                return 0
            lax.fori_loop(0, COLS, one, 0)
        return 0

    lax.fori_loop(0, 2, own, 0)

    def plan(n, _):
        f, p = n >> 1, n & 1
        sx, sy, sh = (either(p, [place[i] for place in places]) for i in range(3))
        home = half == sh
        turn, other = f & 3, f >> 2
        rx, ry = (x - sx) & 3, (y - sy) & 3
        nx, ny = -rx & 3, -ry & 3

        def turned(a, b, c, d):
            return jnp.where(turn == 0, a, jnp.where(turn == 1, b, jnp.where(turn == 2, c, d)))

        place = turned(rx, ry, nx, ny) * 4 + turned(ry, nx, ny, rx)

        def pick(part, i):
            away = jnp.where(other == 0, AWAY[0][part][i], AWAY[1][part][i])
            return bit(jnp.where(home, HOME[part][i], away), place)

        word = 0
        for way in range(4):
            word = word + (pick(0, way) << ((way + turn) & 3))
        gate = jnp.where(other == 0, GATES[0], GATES[1])
        word = word + jnp.where(home & (place == gate), 16, 0)
        late = SKEW * sum(pick(1, i) << i for i in range(4)) + other
        lates[n] = late
        words[n] = word
        return 0

    lax.fori_loop(0, 2 * NF, plan, 0)
    inner = jnp.where((run > 0) & (run < 3), 1, 0)
    pl.semaphore_wait(barrier, 7 + inner)

    def step(s, _):
        def stream(n, _):
            left = s - lates[n]

            @pl.when((left & ~(period * (PIECES - 1))) == 0)
            def _():
                f, p = n >> 1, n & 1
                k = left >> shift
                word = words[n]
                copy(p, f, k, 0).wait_recv()
                pltpu.make_async_copy(piece(p, f, k), rows_hbm.at[p, f, k], out_sem).start()
                for way in range(5):
                    @pl.when((word & (1 << way)) != 0)
                    def _(way=way):
                        copy(p, f, k, way).start()
            return 0

        lax.fori_loop(0, 2 * NF, stream, 0)

        def column(p, _):
            far, goes = col_part(p)
            i = s - 1 - 4 * far

            @pl.when(goes[2] & (i >= 0) & (i < COLS))
            def _():
                col_copy(p, i, 2).wait_recv()
                for way in range(3):
                    @pl.when(goes[way])
                    def _(way=way):
                        col_copy(p, i, way).start()
            return 0

        lax.fori_loop(0, 2, column, 0)
        return 0

    lax.fori_loop(0, period * PIECES + 8 * SKEW + 1, step, 0)

    pltpu.make_async_copy(rows, rows_hbm, out_sem).wait()
    def rest(p, _):
        goes = col_part(p)[1]

        @pl.when(jnp.logical_not(goes[2]))
        def _():
            def one(i, _):
                col_copy(p, i, 2).wait_recv()
                return 0
            lax.fori_loop(0, COLS, one, 0)

        for way in range(3):
            @pl.when(goes[way])
            def _(way=way):
                pltpu.make_async_remote_copy(
                    src_ref=cols.at[p], dst_ref=cols.at[p],
                    send_sem=col_send.at[p, way], recv_sem=col_recv.at[p, 0],
                    device_id=col_ways[2], device_id_type=MESH,
                ).wait_send()
        return 0

    lax.fori_loop(0, 2, rest, 0)

    def sent(n, _):
        f, p = n >> 1, n & 1
        word = words[n]
        for way in range(5):
            @pl.when((word & (1 << way)) != 0)
            def _(way=way):
                pltpu.make_async_remote_copy(
                    src_ref=rows.at[p, f], dst_ref=rows.at[p, f],
                    send_sem=row_send.at[p, f, way], recv_sem=row_recv.at[p, f, 0],
                    device_id=ways[way], device_id_type=MESH,
                ).wait_send()
        return 0

    lax.fori_loop(0, 2 * NF, sent, 0)


def gather(block, data):
    vmem, hbm = (pl.BlockSpec(memory_space=m) for m in (pltpu.VMEM, pltpu.HBM))
    landing = (2, NF, PIECES) + PIECE
    return pl.pallas_call(
        functools.partial(gather_kernel, block),
        out_shape=(
            jax.ShapeDtypeStruct(landing, data.dtype),
            jax.ShapeDtypeStruct((2,) + data.shape[:3] + (SIDE,), data.dtype),
        ),
        in_specs=[hbm],
        out_specs=(hbm, vmem),
        scratch_shapes=[
            pltpu.VMEM(landing, data.dtype),
            pltpu.SMEM((2 * NF,), jnp.int32),
            pltpu.SMEM((2 * NF,), jnp.int32),
            pltpu.SemaphoreType.DMA,
            pltpu.SemaphoreType.DMA((2, NF, PIECES)),
            pltpu.SemaphoreType.DMA((2, NF, 5)),
            pltpu.SemaphoreType.DMA((2, COLS)),
            pltpu.SemaphoreType.DMA((2, 3)),
        ],
        compiler_params=pltpu.CompilerParams(
            collective_id=block, has_side_effects=True, vmem_limit_bytes=16 * 2**20
        ),
        name="gather",
    )(data)


def transform(re, im):
    def c(n):
        return math.cos(math.pi * n / 8)

    def s(n):
        return math.sin(math.pi * n / 8)

    a = c(2)
    quarter = []
    for t in range(4):
        main = (re[4], -im[4], -re[4], im[4])[t]
        last = re[8] if t % 2 == 0 else -re[8]
        quarter.append(main + last - im[8] * s(8 * t))
    d, e = a * (re[2] - re[6]), a * (im[2] + im[6])
    anti = [re[2] + re[6], d - e, im[6] - im[2], -d - e]
    even = [quarter[t] + anti[t] for t in range(4)] + [quarter[t] - anti[t] for t in range(4)]
    p1, q1, p3, q3 = re[1] + re[7], im[1] - im[7], re[3] + re[5], im[3] - im[5]
    m1, n1, m3, n3 = re[1] - re[7], im[1] + im[7], re[3] - re[5], im[3] + im[5]
    g, h = a * (p1 - p3), a * (q1 + q3)
    u, v = c(1) * m1 + s(1) * m3, s(1) * n1 + c(1) * n3
    w, z = s(1) * m1 - c(1) * m3, c(1) * n1 - s(1) * n3
    odd = [p1 + p3, u - v, g - h, w - z, q3 - q1, -w - z, -g - h, -u - v]
    return [even[t] + odd[t] for t in range(8)] + [even[t] - odd[t] for t in range(8)]


def multiply_kernel(wave, rows_hbm, cols, out, rows, left, product, staged, load_sem, sem):
    loads = []
    for i in range(PIECES // TILES):
        some = pl.ds(i * TILES, TILES)
        loads.append(
            pltpu.make_async_copy(rows_hbm.at[:, :, some], rows.at[:, :, some], load_sem.at[i])
        )
        loads[i].start()

    for f in range(NF):
        for p in range(2):
            lr, li = cols[p, 0, f], cols[p, 1, f]
            left[f, :SIDE, 2 * p * SIDE:(2 * p + 1) * SIDE] = lr
            left[f, :SIDE, (2 * p + 1) * SIDE:(2 * p + 2) * SIDE] = -li
            left[f, SIDE:, 2 * p * SIDE:(2 * p + 1) * SIDE] = li
            left[f, SIDE:, (2 * p + 1) * SIDE:(2 * p + 2) * SIDE] = lr

    width = TILES * LANES
    copies = []
    for i in range(PIECES // TILES):
        loads[i].wait()
        for f in range(NF):
            right = jnp.concatenate(
                [
                    jnp.concatenate([rows[p, f, i * TILES + j, c] for j in range(TILES)], axis=1)
                    for p in range(2)
                    for c in range(2)
                ],
                axis=0,
            )
            product[f] = jnp.dot(left[f], right, preferred_element_type=jnp.float32)

        high = 16

        def tile(h, _, i=i):
            at = pl.ds(pl.multiple_of(h * high, high), high)
            at2 = pl.ds(pl.multiple_of(h * high + SIDE, high), high)
            re, im = [None], [None]
            for f in range(NF):
                pr, pi = product[f, at, :], product[f, at2, :]
                wr, wi = wave[0, f] * NF ** -0.5, wave[1, f] * NF ** -0.5
                re.append(wr * pr - wi * pi)
                im.append(wr * pi + wi * pr)
            for t, sample in enumerate(transform(re, im)):
                staged[i, t, at, :] = sample.astype(staged.dtype)
            return 0

        lax.fori_loop(0, SIDE // high, tile, 0)
        copies.append(
            pltpu.make_async_copy(
                staged.at[i], out.at[:, :, pl.ds(i * width, width)], sem.at[i]
            )
        )
        copies[i].start()
    for copy in copies:
        copy.wait()


def multiply(wave, rows, cols):
    width = TILES * LANES
    vmem, hbm = (pl.BlockSpec(memory_space=m) for m in (pltpu.VMEM, pltpu.HBM))
    return pl.pallas_call(
        multiply_kernel,
        out_shape=jax.ShapeDtypeStruct((2 * NF, SIDE, PIECES * LANES), rows.dtype),
        in_specs=[pl.BlockSpec(memory_space=pltpu.SMEM), hbm, vmem],
        out_specs=hbm,
        scratch_shapes=[
            pltpu.VMEM(rows.shape, rows.dtype),
            pltpu.VMEM((NF, 2 * SIDE, 4 * SIDE), rows.dtype),
            pltpu.VMEM((NF, 2 * SIDE, width), jnp.float32),
            pltpu.VMEM((PIECES // TILES, 2 * NF, SIDE, width), rows.dtype),
            pltpu.SemaphoreType.DMA((PIECES // TILES,)),
            pltpu.SemaphoreType.DMA((PIECES // TILES,)),
        ],
        compiler_params=pltpu.CompilerParams(vmem_limit_bytes=24 * 2**20),
        name="multiply",
    )(wave, rows, cols)


def shards(data, inverse_wavelet, panel_blocks):
    block = jnp.min(panel_blocks)
    rows, cols = lax.switch(block, [functools.partial(gather, b) for b in range(LAST)], data)
    return multiply(inverse_wavelet, rows, cols)


def solution(mesh):
    placed = (P(None, None, "shot", "rcv"), P(), P())
    return jax.shard_map(
        shards, mesh=mesh, in_specs=placed, out_specs=P(None, "shot", "rcv"), check_vma=False
    )
```
